256 devices in a mesh: segment: 4 (over x), bins: 64 (over z, y, core).
Axes of the slice: x: 4, y: 4, z: 8, core: 2. Of those that a mesh axis runs over, the one named last changes fastest.
Arguments:
- cube_train: bfloat16 [2, 512, 2048, 256], P(None, None, ('segment', 'bins')), may hold values from -6 to 6
- cube_apply: bfloat16 [2, 512, 2048, 256], P(None, None, ('segment', 'bins')), may hold values from -6 to 6
- hard_bins: int32 [64], replicated, may hold values from 1 to 511, as said below
- easy_bins: int32 [128], replicated, may hold values from 0 to 510, as said below
- stagger: int32 [64, 2], replicated, may hold values from 0 to 127, as said below
- hard_gates: int32 [64, 512], P('bins'), may hold values from 0 to 2047, as said below
- easy_gates: int32 [128, 512], P('bins'), may hold values from 0 to 2047, as said below
Outputs:
- hard_beams: float32 [64, 2, 2048, 128], P('bins', None, 'segment')
- easy_beams: float32 [128, 2, 2048, 128], P('bins', None, 'segment')
The draws below stay inside these ranges and needn't reach their ends.
Inputs may be any that keep to these rules, and one draw needn't show every extreme that they name: `hard_bins`: 64 distinct bins, none of them among easy_bins. `easy_bins`: 128 distinct bins, none of them among hard_bins. `stagger`: in each row the second offset is larger than the first. `hard_gates`: each row holds 512 distinct range gates. `easy_gates`: each row holds 512 distinct range gates.
All inputs are finite; a program needn't handle non-finite values.
Results may differ from the reference program's by a relative error of at most 0.005.
Values may be sent and summed in bfloat16 or wider, within the bound.
No kernel may reach another device: no remote copies, remote signals or barrier semaphores. Data moves between devices by JAX's collectives and lax.ppermute only.
A program may use at most 64 MiB of HBM per device.

```python
import jax
import jax.numpy as jnp
from jax import lax

CH = 256
PULSES = 512
BEAMS = 128
STEPS = 6
STAG = 64
RANGES = 2048
TRAIN = 512
HARD = 64
EASY = 128
N_BINS = 64


def bin_order(key):
    return (2 + jax.random.permutation(jax.random.fold_in(key, 11), PULSES - 4)).astype(jnp.int32)


def draw_hard_bins(key, part):
    others = bin_order(key)[:HARD - 2]
    chosen = jnp.concatenate([jnp.array([PULSES - 1, 1], jnp.int32), others])
    return jax.random.permutation(jax.random.fold_in(key, 12), chosen).astype(jnp.int32)


def draw_easy_bins(key, part):
    others = bin_order(key)[HARD - 2:HARD - 2 + EASY - 2]
    chosen = jnp.concatenate([jnp.array([0, PULSES - 2], jnp.int32), others])
    return jax.random.permutation(jax.random.fold_in(key, 13), chosen).astype(jnp.int32)


def draw_stagger(key, part):
    first = jax.random.randint(jax.random.fold_in(key, 21), (HARD,), 0, STAG, dtype=jnp.int32)
    spacing = jax.random.randint(jax.random.fold_in(key, 22), (HARD,), 1, STAG + 1, dtype=jnp.int32)
    top_row = jax.random.randint(jax.random.fold_in(key, 23), (), 0, HARD, dtype=jnp.int32)
    step_row = jax.random.randint(jax.random.fold_in(key, 24), (), 1, HARD, dtype=jnp.int32)
    low_row = (top_row + step_row) % HARD
    rows = jnp.arange(HARD, dtype=jnp.int32)
    first = jnp.where(rows == top_row, STAG - 1, first)
    spacing = jnp.where(rows == top_row, STAG, spacing)
    first = jnp.where(rows == low_row, 0, first)
    return jnp.stack([first, first + spacing], axis=1).astype(jnp.int32)


def gate_lists(key, count):
    keys = jax.random.split(key, count)
    return jax.vmap(lambda single: jax.random.permutation(single, RANGES)[:TRAIN])(keys).astype(jnp.int32)


def draw_hard_gates(key, part):
    return gate_lists(jax.random.fold_in(key, 31), HARD)


def draw_easy_gates(key, part):
    return gate_lists(jax.random.fold_in(key, 41), EASY)


def block_levels(own_key, extent, shards, smallest, high):
    gain, own = 1.0, jax.random.fold_in(own_key, 6)
    for dim, blocks in shards:
        heights = jnp.exp(jax.random.uniform(jax.random.fold_in(own, dim), (blocks,), jnp.float32, smallest / len(shards), high / len(shards)))
        gain = gain * jnp.repeat(heights, extent[dim] // blocks).reshape([-1 if axis == dim else 1 for axis in range(len(extent))])
    return gain


def centred(own_key, dims, deviation, limit, shards=(), held_as=jnp.bfloat16):
    level = block_levels(own_key, dims, shards, -0.22, 0.18) if shards else 1.0
    values = jax.random.normal(own_key, dims, jnp.float32) * deviation * level
    return jnp.minimum(jnp.maximum(values, -limit), limit).astype(held_as)


def setup_inputs(seed: int = 0) -> dict:
    key_of = jax.random.split(jax.random.key(seed), 8)
    return {
        "cube_train": centred(key_of[0], (2, PULSES, RANGES, CH), 1.0, 6.0, ((2, 256),)),
        "cube_apply": centred(key_of[1], (2, PULSES, RANGES, CH), 1.0, 6.0, ((2, 256),)),
        "hard_bins": draw_hard_bins(jax.random.fold_in(key_of[7], 71), 0),
        "easy_bins": draw_easy_bins(jax.random.fold_in(key_of[7], 71), 0),
        "stagger": draw_stagger(jax.random.fold_in(key_of[7], 71), 0),
        "hard_gates": draw_hard_gates(jax.random.fold_in(key_of[7], 71), 0),
        "easy_gates": draw_easy_gates(jax.random.fold_in(key_of[7], 71), 0),
    }


LOADING = 0.5
TWO_PI = 6.283185307179586

def doppler_table(hard_bins, easy_bins, stagger, pulses, groups):
    zeros = jnp.zeros((groups,), jnp.int32)
    bin_row = jnp.stack([hard_bins, hard_bins, easy_bins[0::2], easy_bins[1::2]], axis=1).reshape(-1)
    offset_row = jnp.stack([stagger[:, 0], stagger[:, 1], zeros, zeros], axis=1).reshape(-1)
    pulse = jnp.arange(pulses, dtype=jnp.int32)
    lagged = pulse[None, :] - offset_row[:, None]
    valid = lagged >= 0
    lagged = jnp.where(valid, lagged, 0).astype(jnp.int32)
    phase = (bin_row[:, None] * lagged % pulses).astype(jnp.float32) * (TWO_PI / pulses)
    taper = 0.54 - 0.46 * jnp.cos(lagged.astype(jnp.float32) * (TWO_PI / pulses))
    amplitude = jnp.where(valid, taper, jnp.zeros_like(taper)) * 0.0625
    real_part = amplitude * jnp.cos(phase)
    imag_part = -amplitude * jnp.sin(phase)
    upper = jnp.concatenate([real_part, -imag_part], axis=1)
    lower = jnp.concatenate([imag_part, real_part], axis=1)
    return jnp.concatenate([upper, lower], axis=0).astype(jnp.bfloat16)

def steering(beam_index, bin_value, offsets, channels, beams, pulses):
    channel = jnp.arange(channels, dtype=jnp.int32)
    spatial = (channel[:, None] * (beam_index[None, :] + beams // 2) % beams).astype(jnp.float32) * (TWO_PI / beams)
    angles = []
    for offset in offsets:
        temporal = (bin_value * offset % pulses).astype(jnp.float32) * (TWO_PI / pulses)
        angles.append(spatial + temporal)
    angle = jnp.concatenate(angles, axis=0)
    scale = 1.0 / jnp.sqrt(jnp.float32(len(offsets) * channels))
    return jnp.concatenate([jnp.cos(angle), jnp.sin(angle)], axis=0) * scale

def chebyshev_solve(snapshot, steer, steps):
    train = snapshot.shape[0]
    order = snapshot.shape[1] // 2
    gram = jnp.dot(snapshot.T, snapshot, preferred_element_type=jnp.float32)
    real_cov = (gram[:order, :order] + gram[order:, order:]) / train
    imag_cov = (gram[:order, order:] - gram[order:, :order]) / train
    trace = jnp.trace(real_cov)
    loading = LOADING * trace / order
    upper = jnp.concatenate([real_cov, -imag_cov], axis=1)
    lower = jnp.concatenate([imag_cov, real_cov], axis=1)
    operator = jnp.concatenate([upper, lower], axis=0) + loading * jnp.eye(2 * order, dtype=gram.dtype)
    lowest = loading
    highest = loading + trace
    theta = (highest + lowest) / 2.0
    delta = (highest - lowest) / 2.0
    sigma = theta / delta
    rho = 1.0 / sigma
    weights = jnp.zeros_like(steer)
    resid = steer
    direction = steer / theta
    for step in range(steps):
        weights = weights + direction
        resid = resid - jnp.dot(operator, direction, precision=lax.Precision.HIGHEST)
        if step + 1 < steps:
            rho_next = 1.0 / (2.0 * sigma - rho)
            direction = rho_next * rho * direction + 2.0 * rho_next / delta * resid
            rho = rho_next
    return weights

def group_weights(snap, hard_bin, offsets, beam_index, channels, beams, pulses, steps):
    train = snap.shape[2]
    hard_snap = jnp.transpose(snap[:, 0:2], (2, 0, 1, 3)).reshape(train, 4 * channels)
    hard_steer = steering(beam_index, hard_bin, offsets, channels, beams, pulses)
    hard_w = chebyshev_solve(hard_snap, hard_steer, steps).astype(jnp.bfloat16)
    parts = [hard_w.reshape(2, 2, channels, -1)]
    zero_offset = jnp.zeros((), jnp.int32)
    easy_steer = steering(beam_index, hard_bin, [zero_offset], channels, beams, pulses)
    for kind in (2, 3):
        easy_snap = jnp.transpose(snap[:, kind], (1, 0, 2)).reshape(train, 2 * channels)
        easy_w = chebyshev_solve(easy_snap, easy_steer, steps).astype(jnp.bfloat16)
        parts.append(easy_w.reshape(2, 1, channels, -1))
    return jnp.concatenate(parts, axis=1)

def beamform(spectra, weights):
    spectra = spectra.astype(jnp.float32)
    weights = weights.astype(jnp.float32)
    swapped = jnp.stack([spectra[1], -spectra[0]])
    stacked = jnp.stack([spectra, swapped])
    hard_part = jnp.einsum('ozkrc,zkcb->orb', stacked[:, :, 0:2], weights[:, 0:2])
    easy_first = jnp.einsum('ozrc,zcb->orb', stacked[:, :, 2], weights[:, 2])
    easy_second = jnp.einsum('ozrc,zcb->orb', stacked[:, :, 3], weights[:, 3])
    return jnp.stack([hard_part, easy_first, easy_second])

def spectra_of(table, cube):
    flat = cube.reshape(2 * PULSES, -1).astype(jnp.float32)
    spectra = jnp.dot(table.astype(jnp.float32), flat, precision=lax.Precision.HIGHEST)
    return spectra.astype(jnp.bfloat16).reshape(2, N_BINS, 4, RANGES, CH)

def reference(cube_train, cube_apply, hard_bins, easy_bins, stagger, hard_gates, easy_gates):
    table = doppler_table(hard_bins, easy_bins, stagger, PULSES, N_BINS)
    spectra_train = spectra_of(table, cube_train)
    spectra_apply = spectra_of(table, cube_apply)
    beam_index = jnp.arange(BEAMS, dtype=jnp.int32)

    def per_group(group_index):
        train_group = lax.dynamic_index_in_dim(spectra_train, group_index, axis=1, keepdims=False)
        apply_group = lax.dynamic_index_in_dim(spectra_apply, group_index, axis=1, keepdims=False)
        easy_rows = lax.dynamic_slice_in_dim(easy_gates, 2 * group_index, 2, 0)
        gate_rows = jnp.concatenate([hard_gates[group_index][None], hard_gates[group_index][None], easy_rows], axis=0)
        snap = jnp.stack([train_group[:, kind][:, gate_rows[kind], :] for kind in range(4)], axis=1)
        offsets = [stagger[group_index, 0], stagger[group_index, 1]]
        weights = group_weights(snap, hard_bins[group_index], offsets, beam_index, CH, BEAMS, PULSES, STEPS)
        return beamform(apply_group, weights)
    outputs = lax.map(per_group, jnp.arange(N_BINS, dtype=jnp.int32))
    hard_beams = outputs[:, 0]
    easy_beams = outputs[:, 1:3].reshape(2 * N_BINS, 2, RANGES, BEAMS)
    return (hard_beams, easy_beams)
```

```python
import functools

import jax
import jax.numpy as jnp
from jax import lax
from jax.experimental import pallas as pl
from jax.experimental.pallas import tpu as pltpu
from jax.sharding import PartitionSpec as P

BEAMS = 128
STEPS = 6
LOADING = 0.5
TWO_PI = 6.283185307179586
MIB = 1024 * 1024


def params(mib):
    return pltpu.CompilerParams(vmem_limit_bytes=mib * MIB)


def vmem():
    return pl.BlockSpec(memory_space=pltpu.VMEM)


def turned(c, s, quarter):
    odd = (quarter & 1) == 1
    a = jnp.where(odd, -s, c)
    b = jnp.where(odd, c, s)
    flip = quarter >= 2
    return jnp.where(flip, -a, a), jnp.where(flip, -b, b)


def doppler_table(hard_bins, easy_bins, stagger, pulses, groups):
    zeros = jnp.zeros((groups,), jnp.int32)
    k = jnp.stack([hard_bins, hard_bins, easy_bins[0::2], easy_bins[1::2]], axis=1)
    d = jnp.stack([stagger[:, 0], stagger[:, 1], zeros, zeros], axis=1)
    k = k.reshape(-1, 1)
    d = d.reshape(-1, 1)
    part = pulses // 4
    lag = jnp.arange(part, dtype=jnp.int32)[None, :] - d
    phase = ((k * lag) & (pulses - 1)).astype(jnp.float32) * (TWO_PI / pulses)
    c0, s0 = jnp.cos(phase), jnp.sin(phase)
    window = lag.astype(jnp.float32) * (TWO_PI / pulses)
    wc, ws = jnp.cos(window), jnp.sin(window)
    window_cos = [wc, -ws, -wc, ws]
    real, imag = [], []
    for a in range(4):
        taper = 0.54 - 0.46 * window_cos[a]
        amplitude = jnp.where(lag + a * part >= 0, taper, 0.0) * 0.0625
        c, s = turned(c0, s0, (k * a) & 3)
        real.append((amplitude * c).astype(jnp.bfloat16))
        imag.append((-amplitude * s).astype(jnp.bfloat16))
    real = jnp.concatenate(real, axis=1)
    imag = jnp.concatenate(imag, axis=1)
    first = jnp.concatenate([real, -imag], axis=1)
    second = jnp.concatenate([imag, real], axis=1)
    return jnp.stack([first, second], axis=1).reshape(-1, 2 * pulses)


def gram_kernel(start_ref, gates_ref, x_ref, hard_ref, easy_ref):
    sources = x_ref.shape[0]
    rows = sources * 16
    row = lax.broadcasted_iota(jnp.int32, (rows, 1), 0)
    gate = (row // 16) * 8 + row % 8 + start_ref[0]
    masks = []
    for which in range(3):
        hit = (gate == gates_ref[which : which + 1, :]).astype(jnp.float32)
        masks.append(jnp.sum(hit, axis=1, keepdims=True))
    plain, masked, turned_ = [], [], []
    for t in range(4):
        x = x_ref[:, t].reshape(rows, -1)
        f = x.astype(jnp.float32)
        f4 = (f * masks[max(t - 1, 0)]).reshape(sources, 2, 8, -1)
        swapped = jnp.concatenate([f4[:, 1:2], -f4[:, 0:1]], axis=1)
        plain.append(x)
        masked.append(f4.reshape(rows, -1).astype(jnp.bfloat16))
        turned_.append(swapped.reshape(rows, -1).astype(jnp.bfloat16))

    def outer(a, b):
        return lax.dot_general(
            a, b, (((0,), (0,)), ((), ())), preferred_element_type=jnp.float32
        )

    def packed(a, m, s):
        order = a.shape[1]
        real, imag = outer(a, m), outer(a, s)
        up = lax.broadcasted_iota(jnp.int32, (order, order), 0) <= lax.broadcasted_iota(
            jnp.int32, (order, order), 1
        )
        return jnp.where(up, real, imag)

    cat = functools.partial(jnp.concatenate, axis=1)
    hard_ref[...] = packed(cat(plain[0:2]), cat(masked[0:2]), cat(turned_[0:2]))
    for e in range(2):
        easy_ref[e] = packed(plain[2 + e], masked[2 + e], turned_[2 + e])


def gram(start, gates, x):
    ch = x.shape[-1]
    return pl.pallas_call(
        gram_kernel,
        out_shape=(
            jax.ShapeDtypeStruct((2 * ch, 2 * ch), jnp.float32),
            jax.ShapeDtypeStruct((2, ch, ch), jnp.float32),
        ),
        in_specs=[pl.BlockSpec(memory_space=pltpu.SMEM), vmem(), vmem()],
        out_specs=(vmem(), vmem()),
        compiler_params=params(40),
        cost_estimate=pl.CostEstimate(
            flops=2 * 10**9, bytes_accessed=4 * MIB, transcendentals=0
        ),
    )(start, gates, x)


def split(x):
    high = x.astype(jnp.bfloat16)
    return high, (x - high.astype(jnp.float32)).astype(jnp.bfloat16)


def solve_one(both, steer, train):
    order = both.shape[0]
    row = lax.broadcasted_iota(jnp.int32, (order, order), 0)
    col = lax.broadcasted_iota(jnp.int32, (order, order), 1)
    both = both * (1.0 / train)
    flipped = both.T
    real = jnp.where(row <= col, both, flipped)
    imag = jnp.where(row > col, both, -flipped)
    imag = jnp.where(row == col, 0.0, imag)
    trace = jnp.sum(jnp.where(row == col, both, 0.0))
    loading = LOADING * trace / order
    highest = loading + trace
    theta = (highest + loading) / 2.0
    delta = (highest - loading) / 2.0
    sigma = theta / delta
    rho = 1.0 / sigma
    real_h, real_l = split(real)
    imag_h, imag_l = split(imag)

    def dot(a, b):
        return jnp.dot(a, b, preferred_element_type=jnp.float32)

    def times(ah, al, bh, bl):
        return dot(ah, bh) + (dot(ah, bl) + dot(al, bh))

    half = steer.shape[1] // 2
    weights = jnp.zeros_like(steer)
    resid = steer
    direction = steer / theta
    for step in range(STEPS):
        weights = weights + direction
        if step + 1 < STEPS:
            dh, dl = split(direction)
            rr = times(real_h, real_l, dh, dl)
            ii = times(imag_h, imag_l, dh, dl)
            product = jnp.concatenate(
                [rr[:, :half] - ii[:, half:], rr[:, half:] + ii[:, :half]], axis=1
            )
            resid = resid - (product + loading * direction)
            rho_next = 1.0 / (2.0 * sigma - rho)
            direction = rho_next * rho * direction + (2.0 * rho_next / delta) * resid
            rho = rho_next
    return weights.astype(jnp.bfloat16)


def solve_kernel(hard_ref, easy_ref, hard_steer_ref, easy_steer_ref, out_ref, *, train):
    ch = easy_ref.shape[1]
    w = solve_one(hard_ref[...], hard_steer_ref[...], train)
    out_ref[0] = w[:ch]
    out_ref[1] = w[ch:]
    for e in range(2):
        out_ref[2 + e] = solve_one(easy_ref[e], easy_steer_ref[...], train)


def solve(hard, easy, hard_steer, easy_steer, train):
    ch = easy.shape[1]
    return pl.pallas_call(
        functools.partial(solve_kernel, train=train),
        out_shape=jax.ShapeDtypeStruct((4, ch, 2 * BEAMS), jnp.bfloat16),
        in_specs=[vmem()] * 4,
        out_specs=vmem(),
        compiler_params=params(40),
        cost_estimate=pl.CostEstimate(
            flops=6 * 10**9, bytes_accessed=3 * MIB, transcendentals=0
        ),
    )(hard, easy, hard_steer, easy_steer)


def steering(bin_value, offsets, channels, pulses):
    channel = jnp.arange(channels, dtype=jnp.int32)
    beam = jnp.arange(BEAMS, dtype=jnp.int32)
    spatial = (channel[:, None] * (beam[None, :] + BEAMS // 2) % BEAMS).astype(
        jnp.float32
    ) * (TWO_PI / BEAMS)
    angles = []
    for offset in offsets:
        temporal = (bin_value * offset % pulses).astype(jnp.float32) * (TWO_PI / pulses)
        angles.append(spatial + temporal)
    angle = jnp.concatenate(angles, axis=0)
    scale = 1.0 / jnp.sqrt(jnp.float32(len(offsets) * channels))
    return jnp.concatenate([jnp.cos(angle), jnp.sin(angle)], axis=1) * scale


def beam_kernel(y_ref, w_ref, hard_ref, easy_ref):
    sources = y_ref.shape[0]
    rows = sources * 16

    def product(t):
        y = y_ref[:, t].reshape(rows, -1)
        return jnp.dot(y, w_ref[t], preferred_element_type=jnp.float32)

    def parts(p):
        p = p.reshape(sources, 2, 8, 2 * BEAMS)
        real = p[:, 0, :, :BEAMS] + p[:, 1, :, BEAMS:]
        imag = p[:, 1, :, :BEAMS] - p[:, 0, :, BEAMS:]
        return real.reshape(sources * 8, BEAMS), imag.reshape(sources * 8, BEAMS)

    hard_ref[0, 0], hard_ref[0, 1] = parts(product(0) + product(1))
    for e in range(2):
        easy_ref[e, 0], easy_ref[e, 1] = parts(product(2 + e))


def beams(y, w, blocks=4):
    sources, _, _, ch = y.shape
    step = sources // blocks
    gates = sources * 8
    return pl.pallas_call(
        beam_kernel,
        grid=(blocks,),
        out_shape=(
            jax.ShapeDtypeStruct((1, 2, gates, BEAMS), jnp.float32),
            jax.ShapeDtypeStruct((2, 2, gates, BEAMS), jnp.float32),
        ),
        in_specs=[
            pl.BlockSpec((step, 4, 16, ch), lambda i: (i, 0, 0, 0)),
            pl.BlockSpec((4, ch, 2 * BEAMS), lambda i: (0, 0, 0)),
        ],
        out_specs=(
            pl.BlockSpec((1, 2, step * 8, BEAMS), lambda i: (0, 0, i, 0)),
            pl.BlockSpec((2, 2, step * 8, BEAMS), lambda i: (0, 0, i, 0)),
        ),
        compiler_params=params(24),
        cost_estimate=pl.CostEstimate(
            flops=5 * 10**8, bytes_accessed=4 * MIB, transcendentals=0
        ),
    )(y, w)


def spectra_of(table, cube, groups):
    pulses, gates, ch = cube.shape[1:]
    flat = cube.reshape(2 * pulses, gates * ch)
    out = jnp.dot(table, flat, preferred_element_type=jnp.float32).astype(jnp.bfloat16)
    return out.reshape(groups, 4, 2 * gates, ch)


def route(spectra):
    return lax.all_to_all(spectra, "bins", split_axis=0, concat_axis=0, tiled=True)


def per_device(cube_train, cube_apply, hard_bins, easy_bins, stagger, hard_gates, easy_gates):
    groups = lax.axis_size("bins")
    section = lax.axis_index("segment")
    group = lax.axis_index("bins")
    pulses = cube_train.shape[1]
    ch = cube_train.shape[3]
    table = doppler_table(hard_bins, easy_bins, stagger, pulses, groups)
    train = route(spectra_of(table, cube_train, groups))
    gates = jnp.concatenate([hard_gates, easy_gates], axis=0)
    start = (section * (groups * 8)).reshape(1).astype(jnp.int32)
    apply_spectra = spectra_of(table, cube_apply, groups)
    train, apply_spectra = lax.optimization_barrier((train, apply_spectra))
    routed = route(apply_spectra)
    hard, easy = gram(start, gates, train)
    both = jnp.concatenate([hard.reshape(-1, ch), easy.reshape(-1, ch)], axis=0)
    both = lax.psum(both, "segment")
    cut = hard.size // ch
    hard = both[:cut].reshape(hard.shape)
    easy = both[cut:].reshape(easy.shape)
    bin_value = hard_bins[group]
    hard_steer = steering(bin_value, [stagger[group, 0], stagger[group, 1]], ch, pulses)
    easy_steer = steering(bin_value, [jnp.zeros((), jnp.int32)], ch, pulses)
    w = solve(hard, easy, hard_steer, easy_steer, hard_gates.shape[1])
    return beams(routed, w)


def solution(mesh):
    in_specs = (
        P(None, None, ("segment", "bins"), None),
        P(None, None, ("segment", "bins"), None),
        P(),
        P(),
        P(),
        P("bins", None),
        P("bins", None),
    )
    out_specs = (P("bins", None, "segment", None), P("bins", None, "segment", None))
    return jax.shard_map(
        per_device, mesh=mesh, in_specs=in_specs, out_specs=out_specs, check_vma=False
    )
```

```python
import functools

import jax
import jax.numpy as jnp
from jax import lax
from jax.experimental import pallas as pl
from jax.experimental.pallas import tpu as pltpu
from jax.sharding import PartitionSpec as P

BEAMS = 128
STEPS = 6
LOADING = 0.5
TWO_PI = 6.283185307179586
MIB = 1024 * 1024


def params(mib):
    return pltpu.CompilerParams(vmem_limit_bytes=mib * MIB)


def vmem():
    return pl.BlockSpec(memory_space=pltpu.VMEM)


def turned(c, s, quarter):
    odd = (quarter & 1) == 1
    a = jnp.where(odd, -s, c)
    b = jnp.where(odd, c, s)
    flip = quarter >= 2
    return jnp.where(flip, -a, a), jnp.where(flip, -b, b)


def iota(shape, dim):
    return lax.broadcasted_iota(jnp.int32, shape, dim)


def table_kernel(hard_ref, easy_ref, stagger_ref, out_ref):
    pulses = out_ref.shape[3] // 2
    groups = hard_ref.shape[1]
    rows = 4 * groups
    part = pulses // 4
    group = iota((rows, 1), 0) // 4
    t = iota((rows, 1), 0) % 4

    def picked(ref, index):
        at = iota((rows, ref.shape[1]), 1) == index
        return jnp.sum(jnp.where(at, ref[...], 0), axis=1, keepdims=True)

    k = jnp.where(t < 2, picked(hard_ref, group), picked(easy_ref, 2 * group + t - 2))
    spread = (iota((rows, groups), 1) == iota((rows, groups), 0) // 4).astype(jnp.float32)
    both = jnp.dot(
        spread.astype(jnp.bfloat16),
        stagger_ref[...].astype(jnp.float32).astype(jnp.bfloat16),
        preferred_element_type=jnp.float32,
    ).astype(jnp.int32)
    d = jnp.where(t == 0, both[:, 0:1], jnp.where(t == 1, both[:, 1:2], 0))
    lag = iota((rows, part), 1) - d
    phase = ((k * lag) & (pulses - 1)).astype(jnp.float32) * (TWO_PI / pulses)
    c0, s0 = jnp.cos(phase), jnp.sin(phase)
    window = lag.astype(jnp.float32) * (TWO_PI / pulses)
    wc, ws = jnp.cos(window), jnp.sin(window)
    for a, window_cos in enumerate([wc, -ws, -wc, ws]):
        taper = 0.54 - 0.46 * window_cos
        amplitude = jnp.where(lag + a * part >= 0, taper, 0.0) * 0.0625
        c, s = turned(c0, s0, (k * a) & 3)
        shape = (groups // 8, 32, part)
        real = (amplitude * c).reshape(shape)
        imag = (amplitude * s).reshape(shape)
        low = slice(a * part, (a + 1) * part)
        high = slice(pulses + a * part, pulses + (a + 1) * part)
        out_ref[:, 0, :, low] = real.astype(jnp.bfloat16)
        out_ref[:, 0, :, high] = imag.astype(jnp.bfloat16)
        out_ref[:, 1, :, low] = (-imag).astype(jnp.bfloat16)
        out_ref[:, 1, :, high] = real.astype(jnp.bfloat16)


def doppler_table(hard_bins, easy_bins, stagger, pulses, groups):
    out = pl.pallas_call(
        table_kernel,
        out_shape=jax.ShapeDtypeStruct((groups // 8, 2, 32, 2 * pulses), jnp.bfloat16),
        in_specs=[vmem()] * 3,
        out_specs=vmem(),
        compiler_params=params(24),
        cost_estimate=pl.CostEstimate(
            flops=10**7, bytes_accessed=MIB, transcendentals=200000
        ),
    )(hard_bins.reshape(1, -1), easy_bins.reshape(1, -1), stagger)
    return out.reshape(-1, 2 * pulses)


def gram_kernel(section_ref, gates_ref, x_ref, *refs, train):
    outs, scratch = refs[:-1], refs[-1]
    section = section_ref[0]
    start = section * (x_ref.shape[0] * 8)
    sources = x_ref.shape[0]
    rows = sources * 16
    row = lax.broadcasted_iota(jnp.int32, (rows, 1), 0)
    gate = (row // 16) * 8 + row % 8 + start
    masks = []
    for which in range(3):
        hit = (gate == gates_ref[which : which + 1, :]).astype(jnp.float32)
        masks.append(jnp.sum(hit, axis=1, keepdims=True))
    plain, masked, turned_ = [], [], []
    for t in range(4):
        x = x_ref[:, t].reshape(rows, -1)
        f = x.astype(jnp.float32)
        f4 = (f * masks[max(t - 1, 0)]).reshape(sources, 2, 8, -1)
        swapped = jnp.concatenate([f4[:, 1:2], -f4[:, 0:1]], axis=1)
        plain.append(x)
        masked.append(f4.reshape(rows, -1).astype(jnp.bfloat16))
        turned_.append(swapped.reshape(rows, -1).astype(jnp.bfloat16))

    def outer(a, b):
        return lax.dot_general(
            a, b, (((0,), (0,)), ((), ())), preferred_element_type=jnp.float32
        )

    def packed(a, m, s):
        order = a.shape[1]
        real, imag = outer(a, m), outer(a, s)
        up = lax.broadcasted_iota(jnp.int32, (order, order), 0) <= lax.broadcasted_iota(
            jnp.int32, (order, order), 1
        )
        return (jnp.where(up, real, imag) * (1.0 / train)).astype(jnp.bfloat16)

    cat = functools.partial(jnp.concatenate, axis=1)
    ch = x_ref.shape[-1]
    hard = packed(cat(plain[0:2]), cat(masked[0:2]), cat(turned_[0:2]))
    full = jnp.concatenate(
        [hard[:, :ch], hard[:, ch:]]
        + [packed(plain[2 + e], masked[2 + e], turned_[2 + e]) for e in range(2)],
        axis=0,
    )
    scratch[...] = full.reshape(scratch.shape)
    sections = len(outs)
    for shift, out in enumerate(outs):
        out[...] = scratch[(section + shift) % sections]


def gram(section, gates, x, sections):
    ch = x.shape[-1]
    block = (6 * ch // sections, ch)
    return pl.pallas_call(
        functools.partial(gram_kernel, train=gates.shape[1]),
        out_shape=[jax.ShapeDtypeStruct(block, jnp.bfloat16)] * sections,
        in_specs=[pl.BlockSpec(memory_space=pltpu.SMEM), vmem(), vmem()],
        out_specs=[vmem()] * sections,
        scratch_shapes=[pltpu.VMEM((sections, *block), jnp.bfloat16)],
        compiler_params=params(40),
        cost_estimate=pl.CostEstimate(
            flops=2 * 10**9, bytes_accessed=4 * MIB, transcendentals=0
        ),
    )(section, gates, x)


def split(x):
    high = x.astype(jnp.bfloat16)
    return high, (x - high.astype(jnp.float32)).astype(jnp.bfloat16)


def solve_one(both, steer):
    order = both.shape[0]
    row = lax.broadcasted_iota(jnp.int32, (order, order), 0)
    col = lax.broadcasted_iota(jnp.int32, (order, order), 1)
    flipped = both.T
    real = jnp.where(row <= col, both, flipped)
    imag = jnp.where(row > col, both, -flipped)
    imag = jnp.where(row == col, 0.0, imag)
    trace = jnp.sum(jnp.where(row == col, both, 0.0))
    loading = LOADING * trace / order
    highest = loading + trace
    theta = (highest + loading) / 2.0
    delta = (highest - loading) / 2.0
    sigma = theta / delta
    rho = 1.0 / sigma
    real = real.astype(jnp.bfloat16)
    imag = imag.astype(jnp.bfloat16)

    def dot(a, b):
        return jnp.dot(a, b, preferred_element_type=jnp.float32)

    half = steer.shape[1] // 2
    weights = jnp.zeros_like(steer)
    resid = steer
    direction = steer / theta
    for step in range(STEPS):
        weights = weights + direction
        if step + 1 < STEPS:
            dh, dl = split(direction)
            rr = dot(real, dh) + dot(real, dl)
            ii = dot(imag, dh) + dot(imag, dl)
            product = jnp.concatenate(
                [rr[:, :half] - ii[:, half:], rr[:, half:] + ii[:, :half]], axis=1
            )
            resid = resid - (product + loading * direction)
            rho_next = 1.0 / (2.0 * sigma - rho)
            direction = rho_next * rho * direction + (2.0 * rho_next / delta) * resid
            rho = rho_next
    return weights.astype(jnp.bfloat16)


def solve_kernel(section_ref, *refs):
    parts, (hard_steer_ref, easy_steer_ref, out_ref, scratch) = refs[:-4], refs[-4:]
    sections = len(parts)
    for shift, part in enumerate(parts):
        scratch[(section_ref[0] + sections - shift) % sections] = part[...]
    ch = out_ref.shape[1]
    full = scratch[...].reshape(6 * ch, ch).astype(jnp.float32)
    hard = jnp.concatenate([full[: 2 * ch], full[2 * ch : 4 * ch]], axis=1)
    w = solve_one(hard, hard_steer_ref[...])
    out_ref[0] = w[:ch]
    out_ref[1] = w[ch:]
    for e in range(2):
        easy = full[(4 + e) * ch : (5 + e) * ch]
        out_ref[2 + e] = solve_one(easy, easy_steer_ref[...])


def solve(section, parts, hard_steer, easy_steer):
    ch = parts[0].shape[1]
    return pl.pallas_call(
        solve_kernel,
        out_shape=jax.ShapeDtypeStruct((4, ch, 2 * BEAMS), jnp.bfloat16),
        in_specs=[pl.BlockSpec(memory_space=pltpu.SMEM)] + [vmem()] * (len(parts) + 2),
        out_specs=vmem(),
        scratch_shapes=[pltpu.VMEM((len(parts), *parts[0].shape), jnp.bfloat16)],
        compiler_params=params(40),
        cost_estimate=pl.CostEstimate(
            flops=6 * 10**9, bytes_accessed=3 * MIB, transcendentals=0
        ),
    )(section, *parts, hard_steer, easy_steer)


def steering(bin_value, offsets, channels, pulses):
    channel = jnp.arange(channels, dtype=jnp.int32)
    beam = jnp.arange(BEAMS, dtype=jnp.int32)
    spatial = (channel[:, None] * (beam[None, :] + BEAMS // 2) % BEAMS).astype(
        jnp.float32
    ) * (TWO_PI / BEAMS)
    angles = []
    for offset in offsets:
        temporal = (bin_value * offset % pulses).astype(jnp.float32) * (TWO_PI / pulses)
        angles.append(spatial + temporal)
    angle = jnp.concatenate(angles, axis=0)
    scale = 1.0 / jnp.sqrt(jnp.float32(len(offsets) * channels))
    return jnp.concatenate([jnp.cos(angle), jnp.sin(angle)], axis=1) * scale


def beam_kernel(y_ref, w_ref, hard_ref, easy_ref):
    sources = y_ref.shape[0]
    rows = sources * 16

    def product(t):
        y = y_ref[:, t].reshape(rows, -1)
        return jnp.dot(y, w_ref[t], preferred_element_type=jnp.float32)

    def parts(p):
        p = p.reshape(sources, 2, 8, 2 * BEAMS)
        real = p[:, 0, :, :BEAMS] + p[:, 1, :, BEAMS:]
        imag = p[:, 1, :, :BEAMS] - p[:, 0, :, BEAMS:]
        return real.reshape(sources * 8, BEAMS), imag.reshape(sources * 8, BEAMS)

    hard_ref[0, 0], hard_ref[0, 1] = parts(product(0) + product(1))
    for e in range(2):
        easy_ref[e, 0], easy_ref[e, 1] = parts(product(2 + e))


def beams(y, w, blocks=4):
    sources, _, _, ch = y.shape
    step = sources // blocks
    gates = sources * 8
    return pl.pallas_call(
        beam_kernel,
        grid=(blocks,),
        out_shape=(
            jax.ShapeDtypeStruct((1, 2, gates, BEAMS), jnp.float32),
            jax.ShapeDtypeStruct((2, 2, gates, BEAMS), jnp.float32),
        ),
        in_specs=[
            pl.BlockSpec((step, 4, 16, ch), lambda i: (i, 0, 0, 0)),
            pl.BlockSpec((4, ch, 2 * BEAMS), lambda i: (0, 0, 0)),
        ],
        out_specs=(
            pl.BlockSpec((1, 2, step * 8, BEAMS), lambda i: (0, 0, i, 0)),
            pl.BlockSpec((2, 2, step * 8, BEAMS), lambda i: (0, 0, i, 0)),
        ),
        compiler_params=params(24),
        cost_estimate=pl.CostEstimate(
            flops=5 * 10**8, bytes_accessed=4 * MIB, transcendentals=0
        ),
    )(y, w)


def spectra_of(table, cube, groups):
    pulses, gates, ch = cube.shape[1:]
    flat = cube.reshape(2 * pulses, gates * ch)
    out = jnp.dot(table, flat, preferred_element_type=jnp.float32).astype(jnp.bfloat16)
    out = out.reshape(groups // 8, 2, 8, 4, gates, ch)
    return jnp.transpose(out, (0, 2, 3, 1, 4, 5)).reshape(groups, 4, 2 * gates, ch)


def route(spectra):
    return lax.all_to_all(spectra, "bins", split_axis=0, concat_axis=0, tiled=True)


def shifted(x, by):
    size = lax.axis_size("segment")
    return lax.ppermute(x, "segment", [(i, (i + by) % size) for i in range(size)])


def per_device(cube_train, cube_apply, hard_bins, easy_bins, stagger, hard_gates, easy_gates):
    groups = lax.axis_size("bins")
    section = lax.axis_index("segment")
    group = lax.axis_index("bins")
    pulses = cube_train.shape[1]
    ch = cube_train.shape[3]
    table = doppler_table(hard_bins, easy_bins, stagger, pulses, groups)
    train = route(spectra_of(table, cube_train, groups))
    gates = jnp.concatenate([hard_gates, easy_gates], axis=0)
    apply_spectra = spectra_of(table, cube_apply, groups)
    train, apply_spectra = lax.optimization_barrier((train, apply_spectra))
    routed = route(apply_spectra)
    sections = lax.axis_size("segment")
    where = section.reshape(1).astype(jnp.int32)
    parts = gram(where, gates, train, sections)
    arrived = [parts[0]] + [shifted(parts[d], d) for d in range(1, sections)]
    own = sum(p.astype(jnp.float32) for p in arrived).astype(jnp.bfloat16)
    parts = [own] + [shifted(own, d) for d in range(1, sections)]
    bin_value = hard_bins[group]
    hard_steer = steering(bin_value, [stagger[group, 0], stagger[group, 1]], ch, pulses)
    easy_steer = steering(bin_value, [jnp.zeros((), jnp.int32)], ch, pulses)
    w = solve(where, parts, hard_steer, easy_steer)
    return beams(routed, w)


def solution(mesh):
    in_specs = (
        P(None, None, ("segment", "bins"), None),
        P(None, None, ("segment", "bins"), None),
        P(),
        P(),
        P(),
        P("bins", None),
        P("bins", None),
    )
    out_specs = (P("bins", None, "segment", None), P("bins", None, "segment", None))
    return jax.shard_map(
        per_device, mesh=mesh, in_specs=in_specs, out_specs=out_specs, check_vma=False
    )
```

```python
import functools

import jax
import jax.numpy as jnp
from jax import lax
from jax.experimental import pallas as pl
from jax.experimental.pallas import tpu as pltpu
from jax.sharding import PartitionSpec as P

BEAMS = 128
STEPS = 6
LOADING = 0.5
TWO_PI = 6.283185307179586
MIB = 1024 * 1024


def params(mib):
    return pltpu.CompilerParams(vmem_limit_bytes=mib * MIB)


def vmem():
    return pl.BlockSpec(memory_space=pltpu.VMEM)


def turned(c, s, quarter):
    odd = (quarter & 1) == 1
    a = jnp.where(odd, -s, c)
    b = jnp.where(odd, c, s)
    flip = quarter >= 2
    return jnp.where(flip, -a, a), jnp.where(flip, -b, b)


def iota(shape, dim):
    return lax.broadcasted_iota(jnp.int32, shape, dim)


def write_table(hard_ref, easy_ref, stagger_ref, out_ref):
    pulses = out_ref.shape[3] // 2
    groups = hard_ref.shape[1]
    rows = 4 * groups
    part = pulses // 4
    group = iota((rows, 1), 0) // 4
    t = iota((rows, 1), 0) % 4

    def picked(ref, index):
        at = iota((rows, ref.shape[1]), 1) == index
        return jnp.sum(jnp.where(at, ref[...], 0), axis=1, keepdims=True)

    k = jnp.where(t < 2, picked(hard_ref, group), picked(easy_ref, 2 * group + t - 2))
    first, second = picked(stagger_ref.at[0:1], group), picked(stagger_ref.at[1:2], group)
    d = jnp.where(t == 0, first, jnp.where(t == 1, second, 0))
    lag = iota((rows, part), 1) - d
    phase = ((k * lag) & (pulses - 1)).astype(jnp.float32) * (TWO_PI / pulses)
    c0, s0 = jnp.cos(phase), jnp.sin(phase)
    window = lag.astype(jnp.float32) * (TWO_PI / pulses)
    wc, ws = jnp.cos(window), jnp.sin(window)
    for a, window_cos in enumerate([wc, -ws, -wc, ws]):
        taper = 0.54 - 0.46 * window_cos
        amplitude = jnp.where(lag + a * part >= 0, taper, 0.0) * 0.0625
        c, s = turned(c0, s0, (k * a) & 3)
        shape = (groups // 8, 32, part)
        real = (amplitude * c).reshape(shape)
        imag = (amplitude * s).reshape(shape)
        low = slice(a * part, (a + 1) * part)
        high = slice(pulses + a * part, pulses + (a + 1) * part)
        out_ref[:, 0, :, low] = real.astype(jnp.bfloat16)
        out_ref[:, 0, :, high] = imag.astype(jnp.bfloat16)
        out_ref[:, 1, :, low] = (-imag).astype(jnp.bfloat16)
        out_ref[:, 1, :, high] = real.astype(jnp.bfloat16)


PIECES = 8


def front_kernel(
    hard_ref, easy_ref, stagger_ref, x_hbm, out_hbm, table, held, wide, tall, done, sems, out_sems
):
    lines, gates, ch = x_hbm.shape
    piece = lines // PIECES
    copies = []
    for n in range(PIECES):
        at = pl.ds(n * piece, piece)
        copies.append(pltpu.make_async_copy(x_hbm.at[at], held.at[at], sems.at[n]))
        copies[-1].start()
    write_table(hard_ref, easy_ref, stagger_ref, table)
    for n, copy in enumerate(copies):
        copy.wait()
        x = held[n * piece : (n + 1) * piece].astype(jnp.float32)
        x = x.reshape(piece * gates, ch)
        for half in range(ch // 128):
            lanes = slice(half * 128, (half + 1) * 128)
            wide[half, n * piece * gates : (n + 1) * piece * gates] = x[:, lanes]
    factors = table[...].reshape(-1, lines)
    rows = factors.shape[0]
    for g in range(gates):
        x = [wide[half, pl.ds(g, lines, stride=gates), :] for half in range(ch // 128)]
        x = jnp.concatenate(x, axis=1).astype(jnp.bfloat16)
        y = jnp.dot(factors, x, preferred_element_type=jnp.float32)
        for half in range(ch // 128):
            tall[half, pl.ds(g, rows, stride=gates), :] = y[:, half * 128 : (half + 1) * 128]
    for z in range(rows // 64):
        lines_of = slice(z * 64 * gates, (z + 1) * 64 * gates)
        for half in range(ch // 128):
            block = tall[half, lines_of].reshape(2, 8, 4, gates, 128)
            block = jnp.concatenate([block[0], block[1]], axis=2).astype(jnp.bfloat16)
            done[z * 8 : (z + 1) * 8, :, :, half * 128 : (half + 1) * 128] = block
        at = pl.ds(z * 8, 8)
        copies.append(pltpu.make_async_copy(done.at[at], out_hbm.at[at], out_sems.at[z]))
        copies[-1].start()
    for copy in copies[PIECES:]:
        copy.wait()


def spectra_of(hard_bins, easy_bins, stagger, cube):
    pulses, gates, ch = cube.shape[1:]
    groups = hard_bins.shape[0]
    lines = 2 * pulses
    rows = 8 * groups
    return pl.pallas_call(
        front_kernel,
        out_shape=jax.ShapeDtypeStruct((groups, 4, 2 * gates, ch), jnp.bfloat16),
        in_specs=[vmem()] * 3 + [pl.BlockSpec(memory_space=pl.ANY)],
        out_specs=pl.BlockSpec(memory_space=pl.ANY),
        scratch_shapes=[
            pltpu.VMEM((groups // 8, 2, 32, lines), jnp.bfloat16),
            pltpu.VMEM((lines, gates, ch), jnp.bfloat16),
            pltpu.VMEM((ch // 128, lines * gates, 128), jnp.float32),
            pltpu.VMEM((ch // 128, rows * gates, 128), jnp.float32),
            pltpu.VMEM((groups, 4, 2 * gates, ch), jnp.bfloat16),
            pltpu.SemaphoreType.DMA((PIECES,)),
            pltpu.SemaphoreType.DMA((groups // 8,)),
        ],
        compiler_params=params(62),
        cost_estimate=pl.CostEstimate(
            flops=2 * 10**9, bytes_accessed=6 * MIB, transcendentals=200000
        ),
    )(
        hard_bins.reshape(1, -1),
        easy_bins.reshape(1, -1),
        stagger.T,
        cube.reshape(lines, gates, ch),
    )


def gram_kernel(section_ref, gates_ref, x_ref, *refs, train):
    outs, scratch = refs[:-1], refs[-1]
    section = section_ref[0]
    start = section * (x_ref.shape[0] * 8)
    sources = x_ref.shape[0]
    rows = sources * 16
    row = lax.broadcasted_iota(jnp.int32, (rows, 1), 0)
    gate = (row // 16) * 8 + row % 8 + start
    masks = []
    for which in range(3):
        hit = (gate == gates_ref[which : which + 1, :]).astype(jnp.float32)
        masks.append(jnp.sum(hit, axis=1, keepdims=True))
    plain, masked, turned_ = [], [], []
    for t in range(4):
        x = x_ref[:, t].reshape(rows, -1)
        f = x.astype(jnp.float32)
        f4 = (f * masks[max(t - 1, 0)]).reshape(sources, 2, 8, -1)
        swapped = jnp.concatenate([f4[:, 1:2], -f4[:, 0:1]], axis=1)
        plain.append(x)
        masked.append(f4.reshape(rows, -1).astype(jnp.bfloat16))
        turned_.append(swapped.reshape(rows, -1).astype(jnp.bfloat16))

    def outer(a, b):
        return lax.dot_general(
            a, b, (((0,), (0,)), ((), ())), preferred_element_type=jnp.float32
        )

    def packed(a, m, s):
        order = a.shape[1]
        real, imag = outer(a, m), outer(a, s)
        up = lax.broadcasted_iota(jnp.int32, (order, order), 0) <= lax.broadcasted_iota(
            jnp.int32, (order, order), 1
        )
        return (jnp.where(up, real, imag) * (1.0 / train)).astype(jnp.bfloat16)

    cat = functools.partial(jnp.concatenate, axis=1)
    ch = x_ref.shape[-1]
    hard = packed(cat(plain[0:2]), cat(masked[0:2]), cat(turned_[0:2]))
    full = jnp.concatenate(
        [hard[:, :ch], hard[:, ch:]]
        + [packed(plain[2 + e], masked[2 + e], turned_[2 + e]) for e in range(2)],
        axis=0,
    )
    scratch[...] = full.reshape(scratch.shape)
    sections = len(outs)
    for shift, out in enumerate(outs):
        out[...] = scratch[(section + shift) % sections]


def gram(section, gates, x, sections):
    ch = x.shape[-1]
    block = (6 * ch // sections, ch)
    return pl.pallas_call(
        functools.partial(gram_kernel, train=gates.shape[1]),
        out_shape=[jax.ShapeDtypeStruct(block, jnp.bfloat16)] * sections,
        in_specs=[pl.BlockSpec(memory_space=pltpu.SMEM), vmem(), vmem()],
        out_specs=[vmem()] * sections,
        scratch_shapes=[pltpu.VMEM((sections, *block), jnp.bfloat16)],
        compiler_params=params(24),
        cost_estimate=pl.CostEstimate(
            flops=2 * 10**9, bytes_accessed=4 * MIB, transcendentals=0
        ),
    )(section, gates, x)


def split(x):
    high = x.astype(jnp.bfloat16)
    return high, (x - high.astype(jnp.float32)).astype(jnp.bfloat16)


def solve_one(both, steer):
    order = both.shape[0]
    row = lax.broadcasted_iota(jnp.int32, (order, order), 0)
    col = lax.broadcasted_iota(jnp.int32, (order, order), 1)
    flipped = both.T
    real = jnp.where(row <= col, both, flipped)
    imag = jnp.where(row > col, both, -flipped)
    imag = jnp.where(row == col, 0.0, imag)
    trace = jnp.sum(jnp.where(row == col, both, 0.0))
    loading = LOADING * trace / order
    highest = loading + trace
    theta = (highest + loading) / 2.0
    delta = (highest - loading) / 2.0
    sigma = theta / delta
    rho = 1.0 / sigma
    real = real.astype(jnp.bfloat16)
    imag = imag.astype(jnp.bfloat16)

    def dot(a, b):
        return jnp.dot(a, b, preferred_element_type=jnp.float32)

    half = steer.shape[1] // 2
    weights = jnp.zeros_like(steer)
    resid = steer
    direction = steer / theta
    for step in range(STEPS):
        weights = weights + direction
        if step + 1 < STEPS:
            dh, dl = split(direction)
            rr = dot(real, dh) + dot(real, dl)
            ii = dot(imag, dh) + dot(imag, dl)
            product = jnp.concatenate(
                [rr[:, :half] - ii[:, half:], rr[:, half:] + ii[:, :half]], axis=1
            )
            resid = resid - (product + loading * direction)
            rho_next = 1.0 / (2.0 * sigma - rho)
            direction = rho_next * rho * direction + (2.0 * rho_next / delta) * resid
            rho = rho_next
    return weights.astype(jnp.bfloat16)


def solve_kernel(section_ref, *refs):
    parts, (hard_steer_ref, easy_steer_ref, out_ref, scratch) = refs[:-4], refs[-4:]
    sections = len(parts)
    for shift, part in enumerate(parts):
        scratch[(section_ref[0] + sections - shift) % sections] = part[...]
    ch = out_ref.shape[1]
    full = scratch[...].reshape(6 * ch, ch).astype(jnp.float32)
    hard = jnp.concatenate([full[: 2 * ch], full[2 * ch : 4 * ch]], axis=1)
    w = solve_one(hard, hard_steer_ref[...])
    out_ref[0] = w[:ch]
    out_ref[1] = w[ch:]
    for e in range(2):
        easy = full[(4 + e) * ch : (5 + e) * ch]
        out_ref[2 + e] = solve_one(easy, easy_steer_ref[...])


def solve(section, parts, hard_steer, easy_steer):
    ch = parts[0].shape[1]
    return pl.pallas_call(
        solve_kernel,
        out_shape=jax.ShapeDtypeStruct((4, ch, 2 * BEAMS), jnp.bfloat16),
        in_specs=[pl.BlockSpec(memory_space=pltpu.SMEM)] + [vmem()] * (len(parts) + 2),
        out_specs=vmem(),
        scratch_shapes=[pltpu.VMEM((len(parts), *parts[0].shape), jnp.bfloat16)],
        compiler_params=params(24),
        cost_estimate=pl.CostEstimate(
            flops=6 * 10**9, bytes_accessed=3 * MIB, transcendentals=0
        ),
    )(section, *parts, hard_steer, easy_steer)


def steering(bin_value, offsets, channels, pulses):
    channel = jnp.arange(channels, dtype=jnp.int32)
    beam = jnp.arange(BEAMS, dtype=jnp.int32)
    spatial = (channel[:, None] * (beam[None, :] + BEAMS // 2) % BEAMS).astype(
        jnp.float32
    ) * (TWO_PI / BEAMS)
    angles = []
    for offset in offsets:
        temporal = (bin_value * offset % pulses).astype(jnp.float32) * (TWO_PI / pulses)
        angles.append(spatial + temporal)
    angle = jnp.concatenate(angles, axis=0)
    scale = 1.0 / jnp.sqrt(jnp.float32(len(offsets) * channels))
    return jnp.concatenate([jnp.cos(angle), jnp.sin(angle)], axis=1) * scale


def beam_kernel(y_ref, w_ref, hard_ref, easy_ref):
    sources = y_ref.shape[0]
    rows = sources * 16

    def product(t):
        y = y_ref[:, t].reshape(rows, -1)
        return jnp.dot(y, w_ref[t], preferred_element_type=jnp.float32)

    def parts(p):
        p = p.reshape(sources, 2, 8, 2 * BEAMS)
        real = p[:, 0, :, :BEAMS] + p[:, 1, :, BEAMS:]
        imag = p[:, 1, :, :BEAMS] - p[:, 0, :, BEAMS:]
        return real.reshape(sources * 8, BEAMS), imag.reshape(sources * 8, BEAMS)

    hard_ref[0, 0], hard_ref[0, 1] = parts(product(0) + product(1))
    for e in range(2):
        easy_ref[e, 0], easy_ref[e, 1] = parts(product(2 + e))


def beams(y, w, blocks=4):
    sources, _, _, ch = y.shape
    step = sources // blocks
    gates = sources * 8
    return pl.pallas_call(
        beam_kernel,
        grid=(blocks,),
        out_shape=(
            jax.ShapeDtypeStruct((1, 2, gates, BEAMS), jnp.float32),
            jax.ShapeDtypeStruct((2, 2, gates, BEAMS), jnp.float32),
        ),
        in_specs=[
            pl.BlockSpec((step, 4, 16, ch), lambda i: (i, 0, 0, 0)),
            pl.BlockSpec((4, ch, 2 * BEAMS), lambda i: (0, 0, 0)),
        ],
        out_specs=(
            pl.BlockSpec((1, 2, step * 8, BEAMS), lambda i: (0, 0, i, 0)),
            pl.BlockSpec((2, 2, step * 8, BEAMS), lambda i: (0, 0, i, 0)),
        ),
        compiler_params=params(24),
        cost_estimate=pl.CostEstimate(
            flops=5 * 10**8, bytes_accessed=4 * MIB, transcendentals=0
        ),
    )(y, w)


def route(spectra):
    return lax.all_to_all(spectra, "bins", split_axis=0, concat_axis=0, tiled=True)


def shifted(x, by):
    size = lax.axis_size("segment")
    return lax.ppermute(x, "segment", [(i, (i + by) % size) for i in range(size)])


def per_device(cube_train, cube_apply, hard_bins, easy_bins, stagger, hard_gates, easy_gates):
    section = lax.axis_index("segment")
    group = lax.axis_index("bins")
    pulses = cube_train.shape[1]
    ch = cube_train.shape[3]
    bins = (hard_bins, easy_bins, stagger)
    train = route(spectra_of(*bins, cube_train))
    gates = jnp.concatenate([hard_gates, easy_gates], axis=0)
    apply_spectra = spectra_of(*bins, cube_apply)
    train, apply_spectra = lax.optimization_barrier((train, apply_spectra))
    routed = route(apply_spectra)
    sections = lax.axis_size("segment")
    where = section.reshape(1).astype(jnp.int32)
    parts = gram(where, gates, train, sections)
    arrived = [parts[0]] + [shifted(parts[d], d) for d in range(1, sections)]
    own = sum(p.astype(jnp.float32) for p in arrived).astype(jnp.bfloat16)
    parts = [own] + [shifted(own, d) for d in range(1, sections)]
    bin_value = hard_bins[group]
    hard_steer = steering(bin_value, [stagger[group, 0], stagger[group, 1]], ch, pulses)
    easy_steer = steering(bin_value, [jnp.zeros((), jnp.int32)], ch, pulses)
    w = solve(where, parts, hard_steer, easy_steer)
    return beams(routed, w)


def solution(mesh):
    in_specs = (
        P(None, None, ("segment", "bins"), None),
        P(None, None, ("segment", "bins"), None),
        P(),
        P(),
        P(),
        P("bins", None),
        P("bins", None),
    )
    out_specs = (P("bins", None, "segment", None), P("bins", None, "segment", None))
    return jax.shard_map(
        per_device, mesh=mesh, in_specs=in_specs, out_specs=out_specs, check_vma=False
    )
```

```python
import functools

import jax
import jax.numpy as jnp
from jax import lax
from jax.experimental import pallas as pl
from jax.experimental.pallas import tpu as pltpu
from jax.sharding import PartitionSpec as P

BEAMS = 128
STEPS = 6
LOADING = 0.5
TWO_PI = 6.283185307179586
MIB = 1024 * 1024


def params(mib):
    return pltpu.CompilerParams(vmem_limit_bytes=mib * MIB)


def vmem():
    return pl.BlockSpec(memory_space=pltpu.VMEM)


def turned(c, s, quarter):
    odd = (quarter & 1) == 1
    a = jnp.where(odd, -s, c)
    b = jnp.where(odd, c, s)
    flip = quarter >= 2
    return jnp.where(flip, -a, a), jnp.where(flip, -b, b)


def iota(shape, dim):
    return lax.broadcasted_iota(jnp.int32, shape, dim)


def write_table(hard_ref, easy_ref, stagger_ref, out_ref):
    pulses = out_ref.shape[3] // 2
    groups = hard_ref.shape[1]
    rows = 4 * groups
    part = pulses // 4
    group = iota((rows, 1), 0) // 4
    t = iota((rows, 1), 0) % 4

    def picked(ref, index):
        at = iota((rows, ref.shape[1]), 1) == index
        return jnp.sum(jnp.where(at, ref[...], 0), axis=1, keepdims=True)

    k = jnp.where(t < 2, picked(hard_ref, group), picked(easy_ref, 2 * group + t - 2))
    first, second = picked(stagger_ref.at[0:1], group), picked(stagger_ref.at[1:2], group)
    d = jnp.where(t == 0, first, jnp.where(t == 1, second, 0))
    lag = iota((rows, part), 1) - d
    phase = ((k * lag) & (pulses - 1)).astype(jnp.float32) * (TWO_PI / pulses)
    c0, s0 = jnp.cos(phase), jnp.sin(phase)
    window = lag.astype(jnp.float32) * (TWO_PI / pulses)
    wc, ws = jnp.cos(window), jnp.sin(window)
    for a, window_cos in enumerate([wc, -ws, -wc, ws]):
        taper = 0.54 - 0.46 * window_cos
        amplitude = jnp.where(lag + a * part >= 0, taper, 0.0) * 0.0625
        c, s = turned(c0, s0, (k * a) & 3)
        shape = (groups // 8, 32, part)
        real = (amplitude * c).reshape(shape)
        imag = (amplitude * s).reshape(shape)
        low = slice(a * part, (a + 1) * part)
        high = slice(pulses + a * part, pulses + (a + 1) * part)
        out_ref[:, 0, :, low] = real.astype(jnp.bfloat16)
        out_ref[:, 0, :, high] = imag.astype(jnp.bfloat16)
        out_ref[:, 1, :, low] = (-imag).astype(jnp.bfloat16)
        out_ref[:, 1, :, high] = real.astype(jnp.bfloat16)


PIECES = 8


def front_kernel(
    hard_ref, easy_ref, stagger_ref, x_hbm, out_hbm, table, held, wide, tall, done, sems, out_sems
):
    lines, gates, ch = x_hbm.shape
    piece = lines // PIECES
    copies = []
    for n in range(PIECES):
        at = pl.ds(n * piece, piece)
        copies.append(pltpu.make_async_copy(x_hbm.at[at], held.at[at], sems.at[n]))
        copies[-1].start()
    write_table(hard_ref, easy_ref, stagger_ref, table)
    for n, copy in enumerate(copies):
        copy.wait()
        x = held[n * piece : (n + 1) * piece].astype(jnp.float32)
        x = x.reshape(piece * gates, ch)
        for half in range(ch // 128):
            lanes = slice(half * 128, (half + 1) * 128)
            wide[half, n * piece * gates : (n + 1) * piece * gates] = x[:, lanes]
    factors = table[...].reshape(-1, lines)
    rows = factors.shape[0]
    for g in range(gates):
        x = [wide[half, pl.ds(g, lines, stride=gates), :] for half in range(ch // 128)]
        x = jnp.concatenate(x, axis=1).astype(jnp.bfloat16)
        y = jnp.dot(factors, x, preferred_element_type=jnp.float32)
        for half in range(ch // 128):
            tall[half, pl.ds(g, rows, stride=gates), :] = y[:, half * 128 : (half + 1) * 128]
    for z in range(rows // 64):
        lines_of = slice(z * 64 * gates, (z + 1) * 64 * gates)
        for half in range(ch // 128):
            block = tall[half, lines_of].reshape(2, 8, 4, gates, 128)
            block = jnp.concatenate([block[0], block[1]], axis=2).astype(jnp.bfloat16)
            done[z * 8 : (z + 1) * 8, :, :, half * 128 : (half + 1) * 128] = block
        at = pl.ds(z * 8, 8)
        copies.append(pltpu.make_async_copy(done.at[at], out_hbm.at[at], out_sems.at[z]))
        copies[-1].start()
    for copy in copies[PIECES:]:
        copy.wait()


def spectra_of(hard_bins, easy_bins, stagger, cube):
    pulses, gates, ch = cube.shape[1:]
    groups = hard_bins.shape[0]
    lines = 2 * pulses
    rows = 8 * groups
    return pl.pallas_call(
        front_kernel,
        out_shape=jax.ShapeDtypeStruct((groups, 4, 2 * gates, ch), jnp.bfloat16),
        in_specs=[vmem()] * 3 + [pl.BlockSpec(memory_space=pl.ANY)],
        out_specs=pl.BlockSpec(memory_space=pl.ANY),
        scratch_shapes=[
            pltpu.VMEM((groups // 8, 2, 32, lines), jnp.bfloat16),
            pltpu.VMEM((lines, gates, ch), jnp.bfloat16),
            pltpu.VMEM((ch // 128, lines * gates, 128), jnp.float32),
            pltpu.VMEM((ch // 128, rows * gates, 128), jnp.float32),
            pltpu.VMEM((groups, 4, 2 * gates, ch), jnp.bfloat16),
            pltpu.SemaphoreType.DMA((PIECES,)),
            pltpu.SemaphoreType.DMA((groups // 8,)),
        ],
        compiler_params=params(62),
        cost_estimate=pl.CostEstimate(
            flops=2 * 10**9, bytes_accessed=6 * MIB, transcendentals=200000
        ),
    )(
        hard_bins.reshape(1, -1),
        easy_bins.reshape(1, -1),
        stagger.T,
        cube.reshape(lines, gates, ch),
    )


def gram_kernel(section_ref, gates_ref, x_ref, *refs, train):
    outs, scratch = refs[:-1], refs[-1]
    section = section_ref[0]
    start = section * (x_ref.shape[0] * 8)
    sources = x_ref.shape[0]
    rows = sources * 16
    row = lax.broadcasted_iota(jnp.int32, (rows, 1), 0)
    gate = (row // 16) * 8 + row % 8 + start
    masks = []
    for which in range(3):
        hit = (gate == gates_ref[which : which + 1, :]).astype(jnp.float32)
        masks.append(jnp.sum(hit, axis=1, keepdims=True))
    plain, masked, turned_ = [], [], []
    for t in range(4):
        x = x_ref[:, t].reshape(rows, -1)
        f = x.astype(jnp.float32)
        f4 = (f * masks[max(t - 1, 0)]).reshape(sources, 2, 8, -1)
        swapped = jnp.concatenate([f4[:, 1:2], -f4[:, 0:1]], axis=1)
        plain.append(x)
        masked.append(f4.reshape(rows, -1).astype(jnp.bfloat16))
        turned_.append(swapped.reshape(rows, -1).astype(jnp.bfloat16))

    def outer(a, b):
        return lax.dot_general(
            a, b, (((0,), (0,)), ((), ())), preferred_element_type=jnp.float32
        )

    def packed(a, m, s):
        order = a.shape[1]
        real, imag = outer(a, m), outer(a, s)
        up = lax.broadcasted_iota(jnp.int32, (order, order), 0) <= lax.broadcasted_iota(
            jnp.int32, (order, order), 1
        )
        return (jnp.where(up, real, imag) * (1.0 / train)).astype(jnp.bfloat16)

    cat = functools.partial(jnp.concatenate, axis=1)
    ch = x_ref.shape[-1]
    hard = packed(cat(plain[0:2]), cat(masked[0:2]), cat(turned_[0:2]))
    full = jnp.concatenate(
        [hard[:, :ch], hard[:, ch:]]
        + [packed(plain[2 + e], masked[2 + e], turned_[2 + e]) for e in range(2)],
        axis=0,
    )
    scratch[...] = full.reshape(scratch.shape)
    sections = len(outs)
    for shift, out in enumerate(outs):
        out[...] = scratch[(section + shift) % sections]


def gram(section, gates, x, sections):
    ch = x.shape[-1]
    block = (6 * ch // sections, ch)
    return pl.pallas_call(
        functools.partial(gram_kernel, train=gates.shape[1]),
        out_shape=[jax.ShapeDtypeStruct(block, jnp.bfloat16)] * sections,
        in_specs=[pl.BlockSpec(memory_space=pltpu.SMEM), vmem(), vmem()],
        out_specs=[vmem()] * sections,
        scratch_shapes=[pltpu.VMEM((sections, *block), jnp.bfloat16)],
        compiler_params=params(24),
        cost_estimate=pl.CostEstimate(
            flops=2 * 10**9, bytes_accessed=4 * MIB, transcendentals=0
        ),
    )(section, gates, x)


def split(x):
    high = x.astype(jnp.bfloat16)
    return high, (x - high.astype(jnp.float32)).astype(jnp.bfloat16)


def solve_one(both, steer):
    order = both.shape[0]
    row = lax.broadcasted_iota(jnp.int32, (order, order), 0)
    col = lax.broadcasted_iota(jnp.int32, (order, order), 1)
    flipped = both.T
    real = jnp.where(row <= col, both, flipped)
    imag = jnp.where(row > col, both, -flipped)
    imag = jnp.where(row == col, 0.0, imag)
    trace = jnp.sum(jnp.where(row == col, both, 0.0))
    loading = LOADING * trace / order
    highest = loading + trace
    theta = (highest + loading) / 2.0
    delta = (highest - loading) / 2.0
    sigma = theta / delta
    rho = 1.0 / sigma
    real = real.astype(jnp.bfloat16)
    imag = imag.astype(jnp.bfloat16)

    def dot(a, b):
        return jnp.dot(a, b, preferred_element_type=jnp.float32)

    half = steer.shape[1] // 2
    weights = jnp.zeros_like(steer)
    resid = steer
    direction = steer / theta
    for step in range(STEPS):
        weights = weights + direction
        if step + 1 < STEPS:
            dh, dl = split(direction)
            rr = dot(real, dh) + dot(real, dl)
            ii = dot(imag, dh) + dot(imag, dl)
            product = jnp.concatenate(
                [rr[:, :half] - ii[:, half:], rr[:, half:] + ii[:, :half]], axis=1
            )
            resid = resid - (product + loading * direction)
            rho_next = 1.0 / (2.0 * sigma - rho)
            direction = rho_next * rho * direction + (2.0 * rho_next / delta) * resid
            rho = rho_next
    return weights.astype(jnp.bfloat16)


def solve_kernel(section_ref, *refs):
    parts, (hard_steer_ref, easy_steer_ref, out_ref, scratch) = refs[:-4], refs[-4:]
    sections = len(parts)
    for shift, part in enumerate(parts):
        scratch[(section_ref[0] + sections - shift) % sections] = part[...]
    ch = out_ref.shape[1]
    full = scratch[...].reshape(6 * ch, ch).astype(jnp.float32)
    hard = jnp.concatenate([full[: 2 * ch], full[2 * ch : 4 * ch]], axis=1)
    w = solve_one(hard, hard_steer_ref[...])
    out_ref[0] = w[:ch]
    out_ref[1] = w[ch:]
    for e in range(2):
        easy = full[(4 + e) * ch : (5 + e) * ch]
        out_ref[2 + e] = solve_one(easy, easy_steer_ref[...])


def solve(section, parts, hard_steer, easy_steer):
    ch = parts[0].shape[1]
    return pl.pallas_call(
        solve_kernel,
        out_shape=jax.ShapeDtypeStruct((4, ch, 2 * BEAMS), jnp.bfloat16),
        in_specs=[pl.BlockSpec(memory_space=pltpu.SMEM)] + [vmem()] * (len(parts) + 2),
        out_specs=vmem(),
        scratch_shapes=[pltpu.VMEM((len(parts), *parts[0].shape), jnp.bfloat16)],
        compiler_params=params(24),
        cost_estimate=pl.CostEstimate(
            flops=6 * 10**9, bytes_accessed=3 * MIB, transcendentals=0
        ),
    )(section, *parts, hard_steer, easy_steer)


def steering(bin_value, offsets, channels, pulses):
    channel = jnp.arange(channels, dtype=jnp.int32)
    beam = jnp.arange(BEAMS, dtype=jnp.int32)
    spatial = (channel[:, None] * (beam[None, :] + BEAMS // 2) % BEAMS).astype(
        jnp.float32
    ) * (TWO_PI / BEAMS)
    angles = []
    for offset in offsets:
        temporal = (bin_value * offset % pulses).astype(jnp.float32) * (TWO_PI / pulses)
        angles.append(spatial + temporal)
    angle = jnp.concatenate(angles, axis=0)
    scale = 1.0 / jnp.sqrt(jnp.float32(len(offsets) * channels))
    return jnp.concatenate([jnp.cos(angle), jnp.sin(angle)], axis=1) * scale


def beam_kernel(y_ref, w_ref, hard_hbm, easy_hbm, hard, easy, sems, *, blocks):
    step = y_ref.shape[0] // blocks
    copies = []

    def parts(p):
        p = p.reshape(step, 2, 8, 2 * BEAMS)
        real = p[:, 0, :, :BEAMS] + p[:, 1, :, BEAMS:]
        imag = p[:, 1, :, :BEAMS] - p[:, 0, :, BEAMS:]
        return real.reshape(step * 8, BEAMS), imag.reshape(step * 8, BEAMS)

    for n in range(blocks):

        def product(t):
            y = y_ref[n * step : (n + 1) * step, t].reshape(step * 16, -1)
            return jnp.dot(y, w_ref[t], preferred_element_type=jnp.float32)

        gates = slice(n * step * 8, (n + 1) * step * 8)
        at = pl.ds(n * step * 8, step * 8)
        hard[0, 0, gates], hard[0, 1, gates] = parts(product(0) + product(1))
        copies.append(
            pltpu.make_async_copy(hard.at[:, :, at], hard_hbm.at[:, :, at], sems.at[0, n])
        )
        copies[-1].start()
        for e in range(2):
            easy[e, 0, gates], easy[e, 1, gates] = parts(product(2 + e))
        copies.append(
            pltpu.make_async_copy(easy.at[:, :, at], easy_hbm.at[:, :, at], sems.at[1, n])
        )
        copies[-1].start()
    for copy in copies:
        copy.wait()


def beams(y, w, blocks=4):
    gates = y.shape[0] * 8
    hard = (1, 2, gates, BEAMS)
    easy = (2, 2, gates, BEAMS)
    return pl.pallas_call(
        functools.partial(beam_kernel, blocks=blocks),
        out_shape=(
            jax.ShapeDtypeStruct(hard, jnp.float32),
            jax.ShapeDtypeStruct(easy, jnp.float32),
        ),
        in_specs=[vmem()] * 2,
        out_specs=(pl.BlockSpec(memory_space=pl.ANY), pl.BlockSpec(memory_space=pl.ANY)),
        scratch_shapes=[
            pltpu.VMEM(hard, jnp.float32),
            pltpu.VMEM(easy, jnp.float32),
            pltpu.SemaphoreType.DMA((2, blocks)),
        ],
        compiler_params=params(24),
        cost_estimate=pl.CostEstimate(
            flops=5 * 10**8, bytes_accessed=4 * MIB, transcendentals=0
        ),
    )(y, w)


def route(spectra):
    return lax.all_to_all(spectra, "bins", split_axis=0, concat_axis=0, tiled=True)


def shifted(x, by):
    size = lax.axis_size("segment")
    return lax.ppermute(x, "segment", [(i, (i + by) % size) for i in range(size)])


def per_device(cube_train, cube_apply, hard_bins, easy_bins, stagger, hard_gates, easy_gates):
    section = lax.axis_index("segment")
    group = lax.axis_index("bins")
    pulses = cube_train.shape[1]
    ch = cube_train.shape[3]
    bins = (hard_bins, easy_bins, stagger)
    train = route(spectra_of(*bins, cube_train))
    gates = jnp.concatenate([hard_gates, easy_gates], axis=0)
    apply_spectra = spectra_of(*bins, cube_apply)
    train, apply_spectra = lax.optimization_barrier((train, apply_spectra))
    routed = route(apply_spectra)
    sections = lax.axis_size("segment")
    where = section.reshape(1).astype(jnp.int32)
    parts = gram(where, gates, train, sections)
    arrived = [parts[0]] + [shifted(parts[d], d) for d in range(1, sections)]
    own = sum(p.astype(jnp.float32) for p in arrived).astype(jnp.bfloat16)
    parts = [own] + [shifted(own, d) for d in range(1, sections)]
    bin_value = hard_bins[group]
    hard_steer = steering(bin_value, [stagger[group, 0], stagger[group, 1]], ch, pulses)
    easy_steer = steering(bin_value, [jnp.zeros((), jnp.int32)], ch, pulses)
    w = solve(where, parts, hard_steer, easy_steer)
    return beams(routed, w)


def solution(mesh):
    in_specs = (
        P(None, None, ("segment", "bins"), None),
        P(None, None, ("segment", "bins"), None),
        P(),
        P(),
        P(),
        P("bins", None),
        P("bins", None),
    )
    out_specs = (P("bins", None, "segment", None), P("bins", None, "segment", None))
    return jax.shard_map(
        per_device, mesh=mesh, in_specs=in_specs, out_specs=out_specs, check_vma=False
    )
```
